32 devices in a mesh: rows: 8 (over z, x), cents: 4 (over y, core).
Axes of the slice: x: 2, y: 2, z: 4, core: 2. Of those that a mesh axis runs over, the one named last changes fastest.
Arguments:
- groups: bfloat16 [65536, 1024], P(('rows', 'cents')), may hold values from -60 to 60
- centroids: bfloat16 [65536, 1024], P(('rows', 'cents')), may hold values from -60 to 60
- row_weight: float32 [65536], P(('rows', 'cents')), may hold values from 0.5 to 18
- block_ids: int32 [256, 8], P(('rows', 'cents')), may hold values from 0 to 511, as said below
- block_counts: int32 [256], P(('rows', 'cents')), may hold values from 1 to 8
Outputs:
- centroid_sums: float32 [65536, 1024], P(('rows', 'cents'))
- column_load: float32 [65536], P(('rows', 'cents'))
The draws below stay inside these ranges and needn't reach their ends.
Inputs may be any that keep to these rules, and one draw needn't show every extreme that they name: `block_ids`: slots k < block_counts[b] are the candidates of row block b; later slots hold valid ids but are unused. List block g is held by the device of index g // 16 in the order rows, then cents. The 8 x 8 slots of the row blocks held by device (r, c) name blocks held by devices (o, c) only, exactly 8 slots for each o, and among those slots exactly 2 distinct blocks of o; the slots of one row block name blocks of distinct holders.
All inputs are finite; a program needn't handle non-finite values.
Results may differ from the reference program's by a relative error of at most 0.0051.
Values may be sent and summed in bfloat16 or wider, within the bound.
A program may use at most 192 MiB of HBM per device.

```python
import math
import jax
import jax.numpy as jnp
from jax import lax

D = 1024
RB = 256
CB = 128
MAXC = 8
USE = 2
ITERS = 3
NBD = 8
CBD = 16
ROWS = 65536
NBLK = 256
K = 65536
N_ROWS = 8
N_CENTS = 4
DEVICES = 32


def scaled_vectors(key, count):
    first, second, third = jax.random.split(key, 3)
    row_factor = jnp.exp(jax.random.uniform(first, (count, 1), jnp.float32, 0.0, math.log(10.0)))
    column_factor = jnp.exp(jax.random.uniform(second, (1, D), jnp.float32, 0.0, math.log(10.0)))
    noise = jnp.clip(jax.random.normal(third, (count, D), jnp.float32), -5.0, 5.0)
    return row_factor * column_factor * noise * 0.1


def draw_groups(key, part):
    return scaled_vectors(jax.random.fold_in(key, 11), ROWS).astype(jnp.bfloat16)


def draw_centroids(key, part):
    return scaled_vectors(jax.random.fold_in(key, 13), K).astype(jnp.bfloat16)


def draw_row_weight(key, part):
    position = jnp.arange(ROWS, dtype=jnp.float32) / (ROWS - 1)
    inner_key = jax.random.fold_in(key, 23)
    base_values = jnp.exp(jax.random.uniform(inner_key, (ROWS,), jnp.float32, math.log(0.5), math.log(2.0)))
    return base_values * (1.0 + 2.0 * position)


def draw_block_ids(key, part):
    device = jnp.arange(DEVICES, dtype=jnp.int32)
    cents_index = device % N_CENTS
    key_list = jax.random.split(jax.random.fold_in(key, 17), DEVICES)

    def holder_order(single_key):
        return jax.random.permutation(single_key, N_ROWS)
    holder_perm = jax.vmap(holder_order)(key_list).astype(jnp.int32)
    choice_keys = jax.random.split(jax.random.fold_in(key, 19), DEVICES * N_ROWS)

    def block_order(single_key):
        return jax.random.permutation(single_key, CBD)[:USE]
    chosen_blocks = jax.vmap(block_order)(choice_keys).astype(jnp.int32).reshape(DEVICES, N_ROWS, USE)
    slot_index = jnp.arange(NBD * MAXC, dtype=jnp.int32)
    holder_row = holder_perm[:, slot_index % N_ROWS]
    reuse_index = slot_index // N_ROWS % USE
    local_block = chosen_blocks[device[:, None], holder_row, reuse_index[None, :]]
    block_list = (holder_row * N_CENTS + cents_index[:, None]) * CBD + local_block
    return block_list.reshape(NBLK, MAXC).astype(jnp.int32)


def plant(drawn, key, smallest, high):
    longest = drawn.shape.index(max(drawn.shape))
    spots = []
    for shift in (0, 1):
        where = [jax.random.randint(jax.random.fold_in(key, axis), (), 0, length) for axis, length in enumerate(drawn.shape)]
        where[longest] = (where[longest] + shift) % drawn.shape[longest]
        spots.append(tuple(where))
    return drawn.at[spots[0]].set(smallest).at[spots[1]].set(high)


def setup_inputs(seed: int = 0) -> dict:
    key_of = jax.random.split(jax.random.key(seed), 6)
    groups = draw_groups(jax.random.fold_in(key_of[5], 71), 0)
    centroids = draw_centroids(jax.random.fold_in(key_of[5], 71), 0)
    row_weight = draw_row_weight(jax.random.fold_in(key_of[5], 71), 0)
    block_ids = draw_block_ids(jax.random.fold_in(key_of[5], 71), 0)
    block_counts = plant(jax.random.randint(key_of[4], (NBLK,), 1, MAXC + 1), jax.random.fold_in(key_of[4], 1), 1, MAXC).astype(jnp.int32)
    return {"groups": groups, "centroids": centroids, "row_weight": row_weight, "block_ids": block_ids, "block_counts": block_counts}


BETA = 32.0
EPSILON = 1e-06
PRIOR = 0.25
HIGHEST = lax.Precision.HIGHEST

def normalize(values):
    widened = values.astype(jnp.float32)
    factor = lax.rsqrt(lax.optimization_barrier(jnp.mean(widened * widened, axis=-1, keepdims=True)) + EPSILON)
    return (widened * factor).astype(jnp.bfloat16)

def reference(groups, centroids, row_weight, block_ids, block_counts):
    blocks_all = block_ids.shape[0]
    lists_blocks = centroids.shape[0] // CB
    rows_norm = normalize(groups).reshape(blocks_all, RB, D)
    lists_norm = normalize(centroids).reshape(lists_blocks, CB, D)
    live_mask = (jnp.arange(MAXC, dtype=jnp.int32)[None, :] < block_counts[:, None]).astype(jnp.float32)

    def kernel_block(operands):
        row_block, block_row, mask_row = operands
        picked_lists = lists_norm[block_row]
        scores = jnp.einsum('rd,kcd->krc', row_block.astype(jnp.float32), picked_lists.astype(jnp.float32))
        return jnp.exp(scores * (BETA / D)) * mask_row[:, None, None]
    kernel = lax.map(kernel_block, (rows_norm, block_ids, live_mask))
    weights = row_weight.reshape(blocks_all, RB)
    target = jnp.sum(row_weight) / (lists_blocks * CB)
    flat_ids = block_ids.reshape(-1)
    scales = jnp.ones((lists_blocks, CB), jnp.float32)

    def row_pass(scales):
        picked = scales[block_ids]
        row_sums = jnp.einsum('bkrc,bkc->br', kernel, picked, precision=HIGHEST)
        return (weights / row_sums, picked)
    for iteration in range(ITERS):
        row_scale, picked = row_pass(scales)
        column_parts = jnp.einsum('bkrc,br->bkc', kernel, row_scale, precision=HIGHEST)
        column = jax.ops.segment_sum(column_parts.reshape(-1, CB), flat_ids, num_segments=lists_blocks)
        scales = target / (column + PRIOR * target)
    row_scale, picked = row_pass(scales)
    transport = row_scale[:, None, :, None] * kernel * picked[:, :, None, :]
    column_mass = jax.ops.segment_sum(lax.optimization_barrier(jnp.sum(transport, axis=2)).reshape(-1, CB), flat_ids, num_segments=lists_blocks)
    transport_half = transport.astype(jnp.bfloat16)

    def accumulate(totals, operands):
        weight_block, row_block, block_row = operands
        list_parts = jnp.einsum('krc,rd->kcd', weight_block.astype(jnp.float32), row_block.astype(jnp.float32))
        return (totals.at[block_row].add(list_parts), None)
    totals, unused = lax.scan(accumulate, jnp.zeros((lists_blocks, CB, D), jnp.float32), (transport_half, rows_norm, block_ids))
    return (totals.reshape(lists_blocks * CB, D), column_mass.reshape(-1) / target)
```

```python
import functools

import jax
import jax.numpy as jnp
from jax import lax
from jax.experimental import pallas as pl
from jax.experimental.pallas import tpu as pltpu
from jax.sharding import PartitionSpec as P

D = 1024
RB = 256
CB = 128
USE = 2
ITERS = 3
BETA = 32.0
EPSILON = 1e-06
PRIOR = 0.25
HIGHEST = lax.Precision.HIGHEST
MESH = pl.DeviceIdType.MESH
F32 = jnp.float32
BF16 = jnp.bfloat16


def normalize(values):
    widened = values.astype(F32)
    factor = lax.rsqrt(jnp.mean(widened * widened, axis=-1, keepdims=True) + EPSILON)
    return (widened * factor).astype(BF16)


def flipped(index, offset):
    result = index
    bit = 1
    while bit <= offset:
        if offset & bit:
            result = result + bit * (1 - 2 * ((index // bit) % 2))
        bit *= 2
    return result


def peer_order(rows_count):
    half = rows_count // 2
    quarter = max(half // 2, 1)
    far = list(range(half + quarter, rows_count)) + list(range(half, half + quarter))
    near = sorted(range(1, half), key=lambda j: -j)
    return [j for j in far if j > 0] + near


def main_kernel(
    rows_count, cents_count, list_total,
    groups, centroids, weights, id_message, id_column, use_table, live_table,
    sums_out, mass_out, ids_out, target_out,
    rows, lists, send, lists_in, kernel, left, weight_column, row_scale,
    ids_scalar, parts, parts_in, scales, match, mass_send, weight_send, weight_in, total,
    load_sem, ids_send_sem, ids_recv_sem, list_send_sem, list_recv_sem, part_send_sem, part_recv_sem,
    sum_send_sem, sum_recv_sem, mass_send_sem, mass_recv_sem, weight_send_sem, weight_recv_sem,
):
    me = lax.axis_index("rows")
    cent = lax.axis_index("cents")
    distinct = rows_count * USE
    list_blocks = lists.shape[0]
    row_blocks = rows.shape[0] // RB
    order = peer_order(rows_count)
    peers = {j: (flipped(me, j), cent) for j in order}
    cent_peers = {q: (me, (cent + q) % cents_count) for q in range(1, cents_count)}

    load_lists = pltpu.make_async_copy(centroids, lists, load_sem.at[0])
    load_lists.start()
    load_rows = pltpu.make_async_copy(groups, rows, load_sem.at[1])
    load_rows.start()

    barrier = pltpu.get_barrier_semaphore()
    for peer in list(peers.values()) + list(cent_peers.values()):
        pl.semaphore_signal(barrier, inc=1, device_id=peer, device_id_type=MESH)
    pl.semaphore_wait(barrier, len(peers) + len(cent_peers))

    def remote(source, target, send_sem, recv_sem, peer):
        copy = pltpu.make_async_remote_copy(
            src_ref=source, dst_ref=target, send_sem=send_sem, recv_sem=recv_sem,
            device_id=peer, device_id_type=MESH,
        )
        copy.start()
        return copy

    id_copies = [
        remote(id_message, ids_out.at[j], ids_send_sem.at[j], ids_recv_sem.at[j], peers[j])
        for j in order
    ]
    ids_out[0] = id_message[...]
    weight_send[...] = jnp.broadcast_to(jnp.sum(weights[...], keepdims=True), weight_send.shape)
    weight_copies = [
        remote(weight_send, weight_in.at[q], weight_send_sem.at[q], weight_recv_sem.at[q], cent_peers[q])
        for q in cent_peers
    ]
    for copy in id_copies:
        copy.wait_recv()
    to_scalar = pltpu.make_async_copy(ids_out, ids_scalar, load_sem.at[2])
    to_scalar.start()
    to_scalar.wait()
    load_lists.wait()

    def normalized_list(j, use):
        wanted = lax.rem(ids_scalar[j, 0, USE * j + use], list_blocks)
        return normalize(lists[wanted])

    list_copies = {}
    for j in order:
        for use in range(USE):
            send[j, use * CB : (use + 1) * CB, :] = normalized_list(j, use)
        list_copies[j] = remote(
            send.at[j], lists_in.at[j], list_send_sem.at[j], list_recv_sem.at[j], peers[j]
        )
    own_ids = [lax.rem(ids_scalar[0, 0, use], list_blocks) for use in range(USE)]
    for use in range(USE):
        lists_in[0, use * CB : (use + 1) * CB, :] = normalize(lists[own_ids[use]])

    load_rows.wait()

    def normalize_rows(index, carry):
        where = pl.ds(pl.multiple_of(index * CB, CB), CB)
        rows[where, :] = normalize(rows[where, :])
        return carry

    lax.fori_loop(0, row_blocks * RB // CB, normalize_rows, 0)

    for index in range(weights.shape[0]):
        spread = jnp.broadcast_to(weights[index : index + 1, :], (128, 128))
        weight_column[index * 128 : (index + 1) * 128, :] = spread.T

    wide = match.shape[1]
    lane = lax.broadcasted_iota(jnp.int32, (1, wide), 1)
    id_row = jnp.zeros((1, wide), jnp.int32)
    for j in range(rows_count):
        id_row = id_row + jnp.where(lane // distinct == j, ids_out[j, 0:1, :], 0)
    match[...] = (id_column[...] == id_row).astype(F32)

    for copy in weight_copies:
        copy.wait_recv()
    group_weight = weight_send[...]
    for q in cent_peers:
        group_weight = group_weight + weight_in[q]
    scales[...] = jnp.ones_like(scales)
    parts[...] = jnp.zeros_like(parts)
    parts[0, distinct : distinct + 8, :] = group_weight

    def scores_of(j):
        def one(block, carry):
            where = pl.ds(pl.multiple_of(block * RB, RB), RB)
            both = lax.dot_general(
                rows[where, :], lists_in[j], (((1,), (1,)), ((), ())), preferred_element_type=F32
            )
            use = use_table[block, j : j + 1, :CB]
            picked = jnp.where(use > 0.5, both[:, CB:], both[:, :CB])
            kernel[block, j] = jnp.exp(picked * (BETA / D)) * live_table[block, j : j + 1, :]
            return carry

        lax.fori_loop(0, row_blocks, one, 0)

    scores_of(0)
    for j in order[::-1]:
        list_copies[j].wait_recv()
        scores_of(j)

    def scale_of(block, j):
        use = use_table[block, j : j + 1, :CB]
        return jnp.where(use > 0.5, scales[USE * j + 1 : USE * j + 2, :], scales[USE * j : USE * j + 1, :])

    def row_step(block):
        total_row = jnp.zeros((RB, CB), F32)
        for j in range(rows_count):
            total_row = total_row + kernel[block, j] * scale_of(block, j)
        where = pl.ds(pl.multiple_of(block * RB, RB), RB)
        return weight_column[where, :] / jnp.sum(total_row, axis=1, keepdims=True)

    part_copies = []
    for step in range(ITERS):
        def column_step(block, carry):
            factor = row_step(block)
            for j in range(rows_count):
                column = jnp.sum(kernel[block, j] * factor, axis=0, keepdims=True)
                use = use_table[block, j : j + 1, :CB]
                low, high = USE * j, USE * j + 1
                parts[step, low : low + 1, :] += column * (1.0 - use)
                parts[step, high : high + 1, :] += column * use
            return carry

        lax.fori_loop(0, row_blocks, column_step, 0)
        copies = [
            remote(
                parts.at[step], parts_in.at[step, j],
                part_send_sem.at[step, j], part_recv_sem.at[step, j], peers[j],
            )
            for j in order
        ]
        parts_in[step, 0] = parts[step]
        for copy in copies:
            copy.wait_recv()
        part_copies += copies
        if step == 0:
            mass = parts_in[0, 0, distinct : distinct + 8, :]
            for j in range(1, rows_count):
                mass = mass + parts_in[0, j, distinct : distinct + 8, :]
            total[...] = mass / list_total
        column_all = jnp.dot(
            match[...],
            parts_in[step, :, :distinct, :].reshape(rows_count * distinct, CB),
            precision=HIGHEST, preferred_element_type=F32,
        )
        target = total[0:1, :]
        scales[...] = target / (column_all + PRIOR * target)

    def last_rows(block, carry):
        where = pl.ds(pl.multiple_of(block * RB, RB), RB)
        row_scale[where, :] = row_step(block)
        return carry

    lax.fori_loop(0, row_blocks, last_rows, 0)
    target_out[...] = total[...]

    sum_copies = []
    mass_copies = []
    keep = []
    for j in order + [0]:
        if j:
            list_copies[j].wait_send()
        mass_send[j] = jnp.zeros((8, CB), F32)

        def transport_of(block, carry):
            where = pl.ds(pl.multiple_of(block * RB, RB), RB)
            transport = row_scale[where, :] * kernel[block, j] * scale_of(block, j)
            column = jnp.sum(transport, axis=0, keepdims=True)
            use = use_table[block, j : j + 1, :]
            mass_send[j, 0:1, :] += column * (1.0 - use[:, :CB])
            mass_send[j, 1:2, :] += column * use[:, :CB]
            turned = transport.T
            left[:CB, where] = jnp.where(use > 0.5, 0.0, turned).astype(BF16)
            left[CB:, where] = jnp.where(use > 0.5, turned, 0.0).astype(BF16)
            return carry

        lax.fori_loop(0, row_blocks, transport_of, 0)

        def product(chunk, carry):
            where = pl.ds(pl.multiple_of(chunk * 256, 256), 256)
            send[j, :, where] = jnp.dot(
                left[...], rows[:, where], preferred_element_type=F32
            ).astype(BF16)
            return carry

        lax.fori_loop(0, D // 256, product, 0)
        if j:
            sum_copies.append(
                remote(send.at[j], sums_out.at[j], sum_send_sem.at[j], sum_recv_sem.at[j], peers[j])
            )
            mass_copies.append(
                remote(
                    mass_send.at[j], mass_out.at[j], mass_send_sem.at[j], mass_recv_sem.at[j], peers[j]
                )
            )
        else:
            mass_out[0] = mass_send[0]
            own = pltpu.make_async_copy(send.at[0], sums_out.at[0], load_sem.at[0])
            own.start()
            keep.append(own)

    for copy in id_copies + weight_copies + part_copies:
        copy.wait_send()
    for copy in mass_copies + sum_copies:
        copy.wait()
    for copy in keep:
        copy.wait()


def combine_kernel(ids, sums, mass, target, out, load):
    block = pl.program_id(0)
    rows_count = sums.shape[0]
    list_blocks = load.shape[0]
    out[...] = jnp.zeros_like(out)
    total = jnp.zeros((1, CB), F32)
    for j in range(rows_count):
        for use in range(USE):
            hit = lax.rem(ids[j, 0, USE * j + use], list_blocks) == block

            @pl.when(hit)
            def _():
                out[...] += sums[j, use * CB : (use + 1) * CB, :].astype(F32)

            total = total + jnp.where(hit, mass[j, use : use + 1, :], 0.0)
    load[pl.ds(block, 1), :] = total / target[0:1, :]


def routing(block_ids, block_counts, list_blocks, rows_count, cents_count):
    holder = block_ids // list_blocks // cents_count
    local = block_ids % list_blocks
    offsets = lax.axis_index("rows") ^ jnp.arange(rows_count, dtype=jnp.int32)
    hit = holder[:, :, None] == offsets[None, None, :]
    slot = jnp.arange(block_ids.shape[1], dtype=jnp.int32)
    alive = slot[None, :] < block_counts[:, None]
    named = jnp.sum(jnp.where(hit, local[:, :, None], 0), axis=1)
    present = jnp.any(hit, axis=1)
    live = jnp.any(hit & alive[:, :, None], axis=1)
    low = jnp.min(jnp.where(present, named, list_blocks), axis=0)
    high = jnp.max(jnp.where(present, named, -1), axis=0)
    use = named == high[None, :]
    ids = offsets[:, None] * list_blocks + jnp.stack([low, high], axis=1)
    return use, live, ids.reshape(-1)


def body(groups, centroids, row_weight, block_ids, block_counts):
    rows_count = lax.axis_size("rows")
    cents_count = lax.axis_size("cents")
    row_blocks = block_ids.shape[0]
    list_blocks = centroids.shape[0] // CB
    list_total = list_blocks * CB * rows_count * cents_count
    distinct = rows_count * USE
    wide = rows_count * distinct
    use, live, ids = routing(block_ids, block_counts, list_blocks, rows_count, cents_count)
    id_message = jnp.broadcast_to(jnp.tile(ids, rows_count)[None, :], (8, wide))
    id_column = jnp.broadcast_to(ids[:, None], (distinct, wide))
    use_table = jnp.broadcast_to(use.astype(F32)[:, :, None], (row_blocks, rows_count, RB))
    live_table = jnp.broadcast_to(live.astype(F32)[:, :, None], (row_blocks, rows_count, CB))
    any_space = pl.BlockSpec(memory_space=pl.ANY)
    vmem = pl.BlockSpec(memory_space=pltpu.VMEM)
    dma = pltpu.SemaphoreType.DMA
    row_total = row_blocks * RB
    sums, mass, all_ids, target = pl.pallas_call(
        functools.partial(main_kernel, rows_count, cents_count, list_total),
        out_shape=(
            jax.ShapeDtypeStruct((rows_count, USE * CB, D), BF16),
            jax.ShapeDtypeStruct((rows_count, 8, CB), F32),
            jax.ShapeDtypeStruct((rows_count, 8, wide), jnp.int32),
            jax.ShapeDtypeStruct((8, CB), F32),
        ),
        in_specs=[any_space, any_space, vmem, vmem, vmem, vmem, vmem],
        out_specs=(any_space, vmem, vmem, vmem),
        scratch_shapes=[
            pltpu.VMEM((row_total, D), BF16),
            pltpu.VMEM((list_blocks, CB, D), BF16),
            pltpu.VMEM((rows_count, USE * CB, D), BF16),
            pltpu.VMEM((rows_count, USE * CB, D), BF16),
            pltpu.VMEM((row_blocks, rows_count, RB, CB), F32),
            pltpu.VMEM((USE * CB, row_total), BF16),
            pltpu.VMEM((row_total, CB), F32),
            pltpu.VMEM((row_total, CB), F32),
            pltpu.SMEM((rows_count, 8, wide), jnp.int32),
            pltpu.VMEM((ITERS, distinct + 8, CB), F32),
            pltpu.VMEM((ITERS, rows_count, distinct + 8, CB), F32),
            pltpu.VMEM((distinct, CB), F32),
            pltpu.VMEM((distinct, wide), F32),
            pltpu.VMEM((rows_count, 8, CB), F32),
            pltpu.VMEM((8, CB), F32),
            pltpu.VMEM((cents_count, 8, CB), F32),
            pltpu.VMEM((8, CB), F32),
            dma((3,)),
            dma((rows_count,)), dma((rows_count,)),
            dma((rows_count,)), dma((rows_count,)),
            dma((ITERS, rows_count)), dma((ITERS, rows_count)),
            dma((rows_count,)), dma((rows_count,)),
            dma((rows_count,)), dma((rows_count,)),
            dma((cents_count,)), dma((cents_count,)),
        ],
        compiler_params=pltpu.CompilerParams(
            collective_id=0, has_side_effects=True, vmem_limit_bytes=56 * 2**20
        ),
        cost_estimate=pl.CostEstimate(
            flops=8 * row_total * D * distinct * CB // 2, bytes_accessed=16 * 2**20, transcendentals=0
        ),
        name="assign",
    )(groups, centroids.reshape(list_blocks, CB, D), row_weight.reshape(-1, 128),
      id_message, id_column, use_table, live_table)
    out, load = pl.pallas_call(
        combine_kernel,
        grid=(list_blocks,),
        out_shape=(
            jax.ShapeDtypeStruct((list_blocks * CB, D), F32),
            jax.ShapeDtypeStruct((list_blocks, CB), F32),
        ),
        in_specs=[
            pl.BlockSpec(memory_space=pltpu.SMEM),
            pl.BlockSpec((rows_count, USE * CB, D), lambda block: (0, 0, 0)),
            pl.BlockSpec((rows_count, 8, CB), lambda block: (0, 0, 0)),
            pl.BlockSpec((8, CB), lambda block: (0, 0)),
        ],
        out_specs=(
            pl.BlockSpec((CB, D), lambda block: (block, 0)),
            pl.BlockSpec((list_blocks, CB), lambda block: (0, 0)),
        ),
        compiler_params=pltpu.CompilerParams(
            dimension_semantics=("arbitrary",), vmem_limit_bytes=48 * 2**20
        ),
        name="combine",
    )(all_ids, sums, mass, target)
    return out, load.reshape(-1)


def solution(mesh):
    placed = (
        P(("rows", "cents"), None),
        P(("rows", "cents"), None),
        P(("rows", "cents")),
        P(("rows", "cents"), None),
        P(("rows", "cents")),
    )
    return jax.shard_map(
        body,
        mesh=mesh,
        in_specs=placed,
        out_specs=(P(("rows", "cents"), None), P(("rows", "cents"))),
        check_vma=False,
    )
```

```python
import functools

import jax
import jax.numpy as jnp
from jax import lax
from jax.experimental import pallas as pl
from jax.experimental.pallas import tpu as pltpu
from jax.sharding import PartitionSpec as P

D = 1024
RB = 256
CB = 128
USE = 2
ITERS = 3
BETA = 32.0
EPSILON = 1e-06
PRIOR = 0.25
HIGHEST = lax.Precision.HIGHEST
MESH = pl.DeviceIdType.MESH
F32 = jnp.float32
BF16 = jnp.bfloat16


def normalize(values):
    widened = values.astype(F32)
    factor = lax.rsqrt(jnp.mean(widened * widened, axis=-1, keepdims=True) + EPSILON)
    return (widened * factor).astype(BF16)


def flipped(index, offset):
    result = index
    bit = 1
    while bit <= offset:
        if offset & bit:
            result = result + bit * (1 - 2 * ((index // bit) % 2))
        bit *= 2
    return result


def peer_order(rows_count):
    half = rows_count // 2
    quarter = half // 2
    far = list(range(half + quarter, rows_count)) + list(range(half, half + quarter))
    return far, list(range(half - 1, 0, -1))


def main_kernel(
    rows_count, cents_count, list_total,
    groups, centroids, weights, block_ids, block_counts,
    sums_out, mass_out, ids_out,
    rows, lists, send, lists_in, kernel, left, weight_column, row_scale,
    id_message, id_column, use_table, live_table, column_parts,
    ids_scalar, parts, parts_in, scales, match, mass_send, weight_send, weight_in, total,
    load_sem, ids_send_sem, ids_recv_sem, list_send_sem, list_recv_sem, part_send_sem, part_recv_sem,
    sum_send_sem, sum_recv_sem, mass_send_sem, mass_recv_sem, weight_send_sem, weight_recv_sem,
):
    me = lax.axis_index("rows")
    cent = lax.axis_index("cents")
    distinct = rows_count * USE
    list_blocks = lists.shape[0]
    row_blocks = rows.shape[0] // RB
    far, near = peer_order(rows_count)
    order = far + near
    peers = {j: (flipped(me, j), cent) for j in order}
    cent_peers = {q: (me, (cent + q) % cents_count) for q in range(1, cents_count)}

    load_lists = pltpu.make_async_copy(centroids, lists, load_sem.at[0])
    load_lists.start()
    load_rows = pltpu.make_async_copy(groups, rows, load_sem.at[1])
    load_rows.start()

    barrier = pltpu.get_barrier_semaphore()
    for peer in list(peers.values()) + list(cent_peers.values()):
        pl.semaphore_signal(barrier, inc=1, device_id=peer, device_id_type=MESH)

    ids = block_ids[...]
    slot = lax.broadcasted_iota(jnp.int32, ids.shape, 1)
    alive = slot < block_counts[...]
    place = lax.broadcasted_iota(jnp.int32, id_message.shape, 1) % distinct
    message = jnp.zeros(id_message.shape, jnp.int32)
    for j in range(rows_count):
        base = (flipped(me, j) * cents_count + cent) * list_blocks
        inside = (ids >= base) & (ids < base + list_blocks)
        named = jnp.max(jnp.where(inside, ids - base, -1), axis=1, keepdims=True)
        live = jnp.max(jnp.where(inside & alive, 1.0, 0.0), axis=1, keepdims=True)
        low = jnp.min(jnp.where(named >= 0, named, list_blocks), axis=0, keepdims=True)
        high = jnp.max(named, axis=0, keepdims=True)
        uses = jnp.broadcast_to((named == high).astype(F32), (row_blocks, RB))
        lives = jnp.broadcast_to(live, (row_blocks, CB))
        for block in range(row_blocks):
            use_table[block, j : j + 1, :] = uses[block : block + 1, :]
            live_table[block, j : j + 1, :] = lives[block : block + 1, :]
        for use, picked in enumerate((low, high)):
            message = jnp.where(place == USE * j + use, base + picked, message)
            row = USE * j + use
            id_column[row : row + 1, :] = jnp.broadcast_to(base + picked, (1, id_column.shape[1]))
    id_message[...] = message

    pl.semaphore_wait(barrier, len(peers) + len(cent_peers))

    def remote(source, target, send_sem, recv_sem, peer):
        copy = pltpu.make_async_remote_copy(
            src_ref=source, dst_ref=target, send_sem=send_sem, recv_sem=recv_sem,
            device_id=peer, device_id_type=MESH,
        )
        copy.start()
        return copy

    id_copies = [
        remote(id_message, ids_out.at[j], ids_send_sem.at[j], ids_recv_sem.at[j], peers[j])
        for j in order
    ]
    ids_out[0] = id_message[...]
    weight_send[...] = jnp.broadcast_to(jnp.sum(weights[...], keepdims=True), weight_send.shape)
    weight_copies = [
        remote(weight_send, weight_in.at[q], weight_send_sem.at[q], weight_recv_sem.at[q], cent_peers[q])
        for q in cent_peers
    ]
    for copy in id_copies:
        copy.wait_recv()
    to_scalar = pltpu.make_async_copy(ids_out, ids_scalar, load_sem.at[2])
    to_scalar.start()
    to_scalar.wait()
    load_lists.wait()

    def normalized_list(j, use):
        wanted = lax.rem(ids_scalar[j, 0, USE * j + use], list_blocks)
        return normalize(lists[wanted])

    list_copies = {}

    def start_lists(j):
        list_copies[j] = remote(
            send.at[j], lists_in.at[j], list_send_sem.at[j], list_recv_sem.at[j], peers[j]
        )

    for j in far[:1] + near + far[1:]:
        for use in range(USE):
            send[j, use * CB : (use + 1) * CB, :] = normalized_list(j, use)
        if j in near or j == far[0]:
            start_lists(j)
    own_ids = [lax.rem(ids_scalar[0, 0, use], list_blocks) for use in range(USE)]
    for use in range(USE):
        lists_in[0, use * CB : (use + 1) * CB, :] = normalize(lists[own_ids[use]])

    load_rows.wait()

    def normalize_rows(index, carry):
        where = pl.ds(pl.multiple_of(index * CB, CB), CB)
        rows[where, :] = normalize(rows[where, :])
        return carry

    lax.fori_loop(0, row_blocks * RB // CB, normalize_rows, 0)

    for index in range(weights.shape[0]):
        spread = jnp.broadcast_to(weights[index : index + 1, :], (128, 128))
        weight_column[index * 128 : (index + 1) * 128, :] = spread.T

    wide = match.shape[1]
    lane = lax.broadcasted_iota(jnp.int32, (1, wide), 1)
    id_row = jnp.zeros((1, wide), jnp.int32)
    for j in range(rows_count):
        id_row = id_row + jnp.where(lane // distinct == j, ids_out[j, 0:1, :], 0)
    match[...] = (id_column[...] == id_row).astype(F32)

    for copy in weight_copies:
        copy.wait_recv()
    group_weight = weight_send[...]
    for q in cent_peers:
        group_weight = group_weight + weight_in[q]
    scales[...] = jnp.ones_like(scales)
    parts[...] = jnp.zeros_like(parts)
    parts[0, distinct : distinct + 8, :] = group_weight

    def scores_of(j):
        def one(block, carry):
            where = pl.ds(pl.multiple_of(block * RB, RB), RB)
            both = lax.dot_general(
                rows[where, :], lists_in[j], (((1,), (1,)), ((), ())), preferred_element_type=F32
            )
            use = use_table[block, j : j + 1, :CB]
            picked = jnp.where(use > 0.5, both[:, CB:], both[:, :CB])
            kernel[block, j] = jnp.exp(picked * (BETA / D)) * live_table[block, j : j + 1, :]
            return carry

        lax.fori_loop(0, row_blocks, one, 0, unroll=2)

    scores_of(0)
    for j in near:
        list_copies[j].wait_recv()
        scores_of(j)
    for index, j in enumerate(far):
        list_copies[j].wait_send()
        if index + 1 < len(far):
            start_lists(far[index + 1])
        list_copies[j].wait_recv()
        scores_of(j)

    def scale_of(block, j):
        use = use_table[block, j : j + 1, :CB]
        return jnp.where(use > 0.5, scales[USE * j + 1 : USE * j + 2, :], scales[USE * j : USE * j + 1, :])

    def row_step(block):
        total_row = jnp.zeros((RB, CB), F32)
        for j in range(rows_count):
            total_row = total_row + kernel[block, j] * scale_of(block, j)
        where = pl.ds(pl.multiple_of(block * RB, RB), RB)
        return weight_column[where, :] / jnp.sum(total_row, axis=1, keepdims=True)

    part_copies = []
    for step in range(ITERS):
        def column_step(block, carry):
            factor = row_step(block)
            for j in range(rows_count):
                column = jnp.sum((kernel[block, j] * factor).reshape(RB // 8, 8, CB), axis=0)
                use = use_table[block, j : j + 1, :CB]
                column_parts[USE * j] += column * (1.0 - use)
                column_parts[USE * j + 1] += column * use
            return carry

        column_parts[...] = jnp.zeros_like(column_parts)
        lax.fori_loop(0, row_blocks, column_step, 0, unroll=2)
        parts[step, :distinct, :] = jnp.sum(column_parts[...], axis=1)
        copies = [
            remote(
                parts.at[step], parts_in.at[step, j],
                part_send_sem.at[step, j], part_recv_sem.at[step, j], peers[j],
            )
            for j in order
        ]
        parts_in[step, 0] = parts[step]
        for copy in copies:
            copy.wait_recv()
        part_copies += copies
        if step == 0:
            mass = parts_in[0, 0, distinct : distinct + 8, :]
            for j in range(1, rows_count):
                mass = mass + parts_in[0, j, distinct : distinct + 8, :]
            total[...] = mass / list_total
        column_all = jnp.dot(
            match[...],
            parts_in[step, :, :distinct, :].reshape(rows_count * distinct, CB),
            precision=HIGHEST, preferred_element_type=F32,
        )
        target = total[0:1, :]
        scales[...] = target / (column_all + PRIOR * target)

    def last_rows(block, carry):
        where = pl.ds(pl.multiple_of(block * RB, RB), RB)
        row_scale[where, :] = row_step(block)
        return carry

    lax.fori_loop(0, row_blocks, last_rows, 0, unroll=2)

    sum_copies = []
    mass_copies = []
    keep = []
    for j in order + [0]:
        if j in near:
            list_copies[j].wait_send()
        mass_send[j] = jnp.zeros((8, CB), F32)

        def transport_of(block, carry):
            where = pl.ds(pl.multiple_of(block * RB, RB), RB)
            transport = row_scale[where, :] * kernel[block, j] * scale_of(block, j)
            column = jnp.sum(transport, axis=0, keepdims=True)
            use = use_table[block, j : j + 1, :]
            mass_send[j, 0:1, :] += column * (1.0 - use[:, :CB])
            mass_send[j, 1:2, :] += column * use[:, :CB]
            turned = transport.T
            left[:CB, where] = jnp.where(use > 0.5, 0.0, turned).astype(BF16)
            left[CB:, where] = jnp.where(use > 0.5, turned, 0.0).astype(BF16)
            return carry

        lax.fori_loop(0, row_blocks, transport_of, 0, unroll=2)
        mass_send[j] = mass_send[j] / total[...]

        def product(chunk, carry):
            where = pl.ds(pl.multiple_of(chunk * 256, 256), 256)
            send[j, :, where] = jnp.dot(
                left[...], rows[:, where], preferred_element_type=F32
            ).astype(BF16)
            return carry

        lax.fori_loop(0, D // 256, product, 0)
        if j:
            sum_copies.append(
                remote(send.at[j], sums_out.at[j], sum_send_sem.at[j], sum_recv_sem.at[j], peers[j])
            )
            mass_copies.append(
                remote(
                    mass_send.at[j], mass_out.at[j], mass_send_sem.at[j], mass_recv_sem.at[j], peers[j]
                )
            )
        else:
            mass_out[0] = mass_send[0]
            own = pltpu.make_async_copy(send.at[0], sums_out.at[0], load_sem.at[0])
            own.start()
            keep.append(own)

    for copy in id_copies + weight_copies + part_copies:
        copy.wait_send()
    for copy in mass_copies + sum_copies:
        copy.wait()
    for copy in keep:
        copy.wait()


def combine_kernel(
    sums, mass, ids, out, load, sums_here, mass_here, ids_scalar, whole, in_sem, out_sem
):
    rows_count = sums.shape[0]
    list_blocks = load.shape[0]
    copies = [
        pltpu.make_async_copy(ids, ids_scalar, in_sem.at[0]),
        pltpu.make_async_copy(mass, mass_here, in_sem.at[1]),
    ]
    copies += [
        pltpu.make_async_copy(sums.at[j], sums_here.at[j], in_sem.at[2 + j]) for j in range(rows_count)
    ]
    for copy in copies:
        copy.start()

    def clear(block, carry):
        whole[block] = jnp.zeros(whole.shape[1:], F32)
        return carry

    lax.fori_loop(0, list_blocks, clear, 0)
    for copy in copies:
        copy.wait()
    local = [
        (j, use, lax.rem(ids_scalar[j, 0, USE * j + use], list_blocks))
        for j in range(rows_count)
        for use in range(USE)
    ]

    def one(block, carry):
        total = jnp.zeros((1, CB), F32)
        for j, use, named in local:
            hit = named == block

            @pl.when(hit)
            def _():
                whole[block] += sums_here[j, use * CB : (use + 1) * CB, :].astype(F32)

            total = total + jnp.where(hit, mass_here[j, use : use + 1, :], 0.0)
        load[pl.ds(block, 1), :] = total
        pltpu.make_async_copy(whole.at[block], out.at[block], out_sem.at[block]).start()
        return carry

    lax.fori_loop(0, list_blocks, one, 0)
    for block in range(list_blocks):
        pltpu.make_async_copy(whole.at[block], out.at[block], out_sem.at[block]).wait()


def body(groups, centroids, row_weight, block_ids, block_counts):
    rows_count = lax.axis_size("rows")
    cents_count = lax.axis_size("cents")
    row_blocks = block_ids.shape[0]
    list_blocks = centroids.shape[0] // CB
    list_total = list_blocks * CB * rows_count * cents_count
    distinct = rows_count * USE
    wide = rows_count * distinct
    count_table = jnp.broadcast_to(block_counts[:, None], block_ids.shape)
    any_space = pl.BlockSpec(memory_space=pl.ANY)
    vmem = pl.BlockSpec(memory_space=pltpu.VMEM)
    dma = pltpu.SemaphoreType.DMA
    row_total = row_blocks * RB
    sums, mass, all_ids = pl.pallas_call(
        functools.partial(main_kernel, rows_count, cents_count, list_total),
        out_shape=(
            jax.ShapeDtypeStruct((rows_count, USE * CB, D), BF16),
            jax.ShapeDtypeStruct((rows_count, 8, CB), F32),
            jax.ShapeDtypeStruct((rows_count, 8, wide), jnp.int32),
        ),
        in_specs=[any_space, any_space, vmem, vmem, vmem],
        out_specs=(any_space, vmem, vmem),
        scratch_shapes=[
            pltpu.VMEM((row_total, D), BF16),
            pltpu.VMEM((list_blocks, CB, D), BF16),
            pltpu.VMEM((rows_count, USE * CB, D), BF16),
            pltpu.VMEM((rows_count, USE * CB, D), BF16),
            pltpu.VMEM((row_blocks, rows_count, RB, CB), F32),
            pltpu.VMEM((USE * CB, row_total), BF16),
            pltpu.VMEM((row_total, CB), F32),
            pltpu.VMEM((row_total, CB), F32),
            pltpu.VMEM((8, wide), jnp.int32),
            pltpu.VMEM((distinct, wide), jnp.int32),
            pltpu.VMEM((row_blocks, rows_count, RB), F32),
            pltpu.VMEM((row_blocks, rows_count, CB), F32),
            pltpu.VMEM((distinct, 8, CB), F32),
            pltpu.SMEM((rows_count, 8, wide), jnp.int32),
            pltpu.VMEM((ITERS, distinct + 8, CB), F32),
            pltpu.VMEM((ITERS, rows_count, distinct + 8, CB), F32),
            pltpu.VMEM((distinct, CB), F32),
            pltpu.VMEM((distinct, wide), F32),
            pltpu.VMEM((rows_count, 8, CB), F32),
            pltpu.VMEM((8, CB), F32),
            pltpu.VMEM((cents_count, 8, CB), F32),
            pltpu.VMEM((8, CB), F32),
            dma((3,)),
            dma((rows_count,)), dma((rows_count,)),
            dma((rows_count,)), dma((rows_count,)),
            dma((ITERS, rows_count)), dma((ITERS, rows_count)),
            dma((rows_count,)), dma((rows_count,)),
            dma((rows_count,)), dma((rows_count,)),
            dma((cents_count,)), dma((cents_count,)),
        ],
        compiler_params=pltpu.CompilerParams(
            collective_id=0, has_side_effects=True, vmem_limit_bytes=56 * 2**20
        ),
        cost_estimate=pl.CostEstimate(
            flops=8 * row_total * D * distinct * CB // 2, bytes_accessed=16 * 2**20, transcendentals=0
        ),
        name="assign",
    )(groups, centroids.reshape(list_blocks, CB, D), row_weight.reshape(-1, 128),
      block_ids, count_table)
    out, load = pl.pallas_call(
        combine_kernel,
        out_shape=(
            jax.ShapeDtypeStruct((list_blocks, CB, D), F32),
            jax.ShapeDtypeStruct((list_blocks, CB), F32),
        ),
        in_specs=[any_space, any_space, any_space],
        out_specs=(any_space, vmem),
        scratch_shapes=[
            pltpu.VMEM((rows_count, USE * CB, D), BF16),
            pltpu.VMEM((rows_count, 8, CB), F32),
            pltpu.SMEM((rows_count, 8, wide), jnp.int32),
            pltpu.VMEM((list_blocks, CB, D), F32),
            dma((2 + rows_count,)),
            dma((list_blocks,)),
        ],
        compiler_params=pltpu.CompilerParams(vmem_limit_bytes=56 * 2**20),
        name="combine",
    )(sums, mass, all_ids)
    return out.reshape(-1, D), load.reshape(-1)


def solution(mesh):
    placed = (
        P(("rows", "cents"), None),
        P(("rows", "cents"), None),
        P(("rows", "cents")),
        P(("rows", "cents"), None),
        P(("rows", "cents")),
    )
    return jax.shard_map(
        body,
        mesh=mesh,
        in_specs=placed,
        out_specs=(P(("rows", "cents"), None), P(("rows", "cents"))),
        check_vma=False,
    )
```

```python
import functools

import jax
import jax.numpy as jnp
from jax import lax
from jax.experimental import pallas as pl
from jax.experimental.pallas import tpu as pltpu
from jax.sharding import PartitionSpec as P

D = 1024
RB = 256
CB = 128
USE = 2
ITERS = 3
BETA = 32.0
EPSILON = 1e-06
PRIOR = 0.25
HIGHEST = lax.Precision.HIGHEST
MESH = pl.DeviceIdType.MESH
F32 = jnp.float32
BF16 = jnp.bfloat16


def normalize(values):
    widened = values.astype(F32)
    factor = lax.rsqrt(jnp.mean(widened * widened, axis=-1, keepdims=True) + EPSILON)
    return (widened * factor).astype(BF16)


def flipped(index, offset):
    result = index
    bit = 1
    while bit <= offset:
        if offset & bit:
            result = result + bit * (1 - 2 * ((index // bit) % 2))
        bit *= 2
    return result


def peer_order(rows_count):
    half = rows_count // 2
    quarter = half // 2
    far = list(range(half + quarter, rows_count)) + list(range(half, half + quarter))
    return far, list(range(half - 1, 0, -1))


def main_kernel(
    rows_count, cents_count, list_total,
    groups, centroids, weights, block_ids, block_counts,
    sums_out, mass_out, ids_out,
    rows, lists, send, lists_in, kernel, left, weight_column, row_scale,
    id_message, id_column, use_table, live_table, column_parts,
    ids_scalar, parts, parts_in, scales, match, mass_send, weight_send, weight_in, total,
    load_sem, ids_send_sem, ids_recv_sem, list_send_sem, list_recv_sem, part_send_sem, part_recv_sem,
    sum_send_sem, sum_recv_sem, mass_send_sem, mass_recv_sem, weight_send_sem, weight_recv_sem,
):
    me = lax.axis_index("rows")
    cent = lax.axis_index("cents")
    distinct = rows_count * USE
    list_blocks = lists.shape[0]
    row_blocks = rows.shape[0] // RB
    far, near = peer_order(rows_count)
    order = far + near
    peers = {j: (flipped(me, j), cent) for j in order}
    cent_peers = {q: (me, (cent + q) % cents_count) for q in range(1, cents_count)}

    load_lists = pltpu.make_async_copy(centroids, lists, load_sem.at[0])
    load_lists.start()
    load_rows = pltpu.make_async_copy(groups, rows, load_sem.at[1])
    load_rows.start()

    barrier = pltpu.get_barrier_semaphore()
    for peer in list(peers.values()) + list(cent_peers.values()):
        pl.semaphore_signal(barrier, inc=1, device_id=peer, device_id_type=MESH)

    ids = block_ids[...]
    slot = lax.broadcasted_iota(jnp.int32, ids.shape, 1)
    block_row = lax.broadcasted_iota(jnp.int32, ids.shape, 0)
    count = jnp.zeros(ids.shape, jnp.int32)
    for block in range(row_blocks):
        count = jnp.where(block_row == block, block_counts[block], count)
    alive = slot < count
    place = lax.broadcasted_iota(jnp.int32, id_message.shape, 1) % distinct
    message = jnp.zeros(id_message.shape, jnp.int32)
    for j in range(rows_count):
        base = (flipped(me, j) * cents_count + cent) * list_blocks
        inside = (ids >= base) & (ids < base + list_blocks)
        named = jnp.max(jnp.where(inside, ids - base, -1), axis=1, keepdims=True)
        live = jnp.max(jnp.where(inside & alive, 1.0, 0.0), axis=1, keepdims=True)
        low = jnp.min(jnp.where(named >= 0, named, list_blocks), axis=0, keepdims=True)
        high = jnp.max(named, axis=0, keepdims=True)
        uses = jnp.broadcast_to((named == high).astype(F32), (row_blocks, RB))
        lives = jnp.broadcast_to(live, (row_blocks, CB))
        for block in range(row_blocks):
            use_table[block, j : j + 1, :] = uses[block : block + 1, :]
            live_table[block, j : j + 1, :] = lives[block : block + 1, :]
        for use, picked in enumerate((low, high)):
            message = jnp.where(place == USE * j + use, base + picked, message)
            row = USE * j + use
            id_column[row : row + 1, :] = jnp.broadcast_to(base + picked, (1, id_column.shape[1]))
    id_message[...] = message

    pl.semaphore_wait(barrier, len(peers) + len(cent_peers))

    def remote(source, target, send_sem, recv_sem, peer):
        copy = pltpu.make_async_remote_copy(
            src_ref=source, dst_ref=target, send_sem=send_sem, recv_sem=recv_sem,
            device_id=peer, device_id_type=MESH,
        )
        copy.start()
        return copy

    id_copies = [
        remote(id_message, ids_out.at[j], ids_send_sem.at[j], ids_recv_sem.at[j], peers[j])
        for j in order
    ]
    ids_out[0] = id_message[...]
    weight_send[...] = jnp.broadcast_to(jnp.sum(weights[...], keepdims=True), weight_send.shape)
    weight_copies = [
        remote(weight_send, weight_in.at[q], weight_send_sem.at[q], weight_recv_sem.at[q], cent_peers[q])
        for q in cent_peers
    ]
    for copy in id_copies:
        copy.wait_recv()
    to_scalar = pltpu.make_async_copy(ids_out.at[:, 0:1, :], ids_scalar, load_sem.at[2])
    to_scalar.start()
    to_scalar.wait()
    load_lists.wait()

    def normalized_list(j, use):
        wanted = lax.rem(ids_scalar[j, 0, USE * j + use], list_blocks)
        return normalize(lists[wanted])

    list_copies = {}

    def start_lists(j):
        list_copies[j] = remote(
            send.at[j], lists_in.at[j], list_send_sem.at[j], list_recv_sem.at[j], peers[j]
        )

    ahead = 2
    for j in far[:ahead] + near + far[ahead:]:
        for use in range(USE):
            send[j, use * CB : (use + 1) * CB, :] = normalized_list(j, use)
        if j in near or j in far[:ahead]:
            start_lists(j)
    own_ids = [lax.rem(ids_scalar[0, 0, use], list_blocks) for use in range(USE)]
    for use in range(USE):
        lists_in[0, use * CB : (use + 1) * CB, :] = normalize(lists[own_ids[use]])

    load_rows.wait()

    def normalize_rows(index, carry):
        where = pl.ds(pl.multiple_of(index * CB, CB), CB)
        rows[where, :] = normalize(rows[where, :])
        return carry

    lax.fori_loop(0, row_blocks * RB // CB, normalize_rows, 0)

    for index in range(weights.shape[0]):
        spread = jnp.broadcast_to(weights[index : index + 1, :], (128, 128))
        weight_column[index * 128 : (index + 1) * 128, :] = spread.T

    wide = match.shape[1]
    lane = lax.broadcasted_iota(jnp.int32, (1, wide), 1)
    id_row = jnp.zeros((1, wide), jnp.int32)
    for j in range(rows_count):
        id_row = id_row + jnp.where(lane // distinct == j, ids_out[j, 0:1, :], 0)
    match[...] = (id_column[...] == id_row).astype(F32)

    for copy in weight_copies:
        copy.wait_recv()
    group_weight = weight_send[...]
    for q in cent_peers:
        group_weight = group_weight + weight_in[q]
    scales[...] = jnp.ones_like(scales)
    parts[...] = jnp.zeros_like(parts)
    parts[0, distinct : distinct + 8, :] = group_weight

    def scores_of(j):
        def one(block, carry):
            where = pl.ds(pl.multiple_of(block * RB, RB), RB)
            both = lax.dot_general(
                rows[where, :], lists_in[j], (((1,), (1,)), ((), ())), preferred_element_type=F32
            )
            use = use_table[block, j : j + 1, :CB]
            picked = jnp.where(use > 0.5, both[:, CB:], both[:, :CB])
            kernel[block, j] = jnp.exp(picked * (BETA / D)) * live_table[block, j : j + 1, :]
            return carry

        lax.fori_loop(0, row_blocks, one, 0, unroll=2)

    scores_of(0)
    for j in near:
        list_copies[j].wait_recv()
        scores_of(j)
    for index, j in enumerate(far):
        list_copies[j].wait_send()
        if index + ahead < len(far):
            start_lists(far[index + ahead])
        list_copies[j].wait_recv()
        scores_of(j)

    def scale_of(block, j):
        use = use_table[block, j : j + 1, :CB]
        return jnp.where(use > 0.5, scales[USE * j + 1 : USE * j + 2, :], scales[USE * j : USE * j + 1, :])

    def row_step(block):
        total_row = jnp.zeros((RB, CB), F32)
        for j in range(rows_count):
            total_row = total_row + kernel[block, j] * scale_of(block, j)
        where = pl.ds(pl.multiple_of(block * RB, RB), RB)
        return weight_column[where, :] / jnp.sum(total_row, axis=1, keepdims=True)

    part_copies = []
    for step in range(ITERS):
        def column_step(block, carry):
            factor = row_step(block)
            for j in range(rows_count):
                column = jnp.sum((kernel[block, j] * factor).reshape(RB // 8, 8, CB), axis=0)
                use = use_table[block, j : j + 1, :CB]
                column_parts[USE * j] += column * (1.0 - use)
                column_parts[USE * j + 1] += column * use
            return carry

        column_parts[...] = jnp.zeros_like(column_parts)
        lax.fori_loop(0, row_blocks, column_step, 0, unroll=2)
        parts[step, :distinct, :] = jnp.sum(column_parts[...], axis=1)
        copies = [
            remote(
                parts.at[step], parts_in.at[step, j],
                part_send_sem.at[step, j], part_recv_sem.at[step, j], peers[j],
            )
            for j in order
        ]
        parts_in[step, 0] = parts[step]
        for copy in copies:
            copy.wait_recv()
        part_copies += copies
        if step == 0:
            mass = parts_in[0, 0, distinct : distinct + 8, :]
            for j in range(1, rows_count):
                mass = mass + parts_in[0, j, distinct : distinct + 8, :]
            total[...] = mass / list_total
        column_all = jnp.dot(
            match[...],
            parts_in[step, :, :distinct, :].reshape(rows_count * distinct, CB),
            precision=HIGHEST, preferred_element_type=F32,
        )
        target = total[0:1, :]
        scales[...] = target / (column_all + PRIOR * target)

    def last_rows(block, carry):
        where = pl.ds(pl.multiple_of(block * RB, RB), RB)
        row_scale[where, :] = row_step(block)
        return carry

    lax.fori_loop(0, row_blocks, last_rows, 0, unroll=2)

    sum_copies = []
    mass_copies = []
    keep = []
    for j in order + [0]:
        if j in near:
            list_copies[j].wait_send()
        mass_send[j] = jnp.zeros((8, CB), F32)

        def transport_of(block, carry):
            where = pl.ds(pl.multiple_of(block * RB, RB), RB)
            transport = row_scale[where, :] * kernel[block, j] * scale_of(block, j)
            column = jnp.sum(transport, axis=0, keepdims=True)
            use = use_table[block, j : j + 1, :]
            mass_send[j, 0:1, :] += column * (1.0 - use[:, :CB])
            mass_send[j, 1:2, :] += column * use[:, :CB]
            turned = transport.T
            left[:CB, where] = jnp.where(use > 0.5, 0.0, turned).astype(BF16)
            left[CB:, where] = jnp.where(use > 0.5, turned, 0.0).astype(BF16)
            return carry

        lax.fori_loop(0, row_blocks, transport_of, 0, unroll=2)
        mass_send[j] = mass_send[j] / total[...]

        def product(chunk, carry):
            where = pl.ds(pl.multiple_of(chunk * 256, 256), 256)
            send[j, :, where] = jnp.dot(
                left[...], rows[:, where], preferred_element_type=F32
            ).astype(BF16)
            return carry

        lax.fori_loop(0, D // 256, product, 0)
        if j:
            sum_copies.append(
                remote(send.at[j], sums_out.at[j], sum_send_sem.at[j], sum_recv_sem.at[j], peers[j])
            )
            mass_copies.append(
                remote(
                    mass_send.at[j], mass_out.at[j], mass_send_sem.at[j], mass_recv_sem.at[j], peers[j]
                )
            )
        else:
            mass_out[0] = mass_send[0]
            own = pltpu.make_async_copy(send.at[0], sums_out.at[0], load_sem.at[0])
            own.start()
            keep.append(own)

    for copy in id_copies + weight_copies + part_copies:
        copy.wait_send()
    for copy in mass_copies + sum_copies:
        copy.wait()
    for copy in keep:
        copy.wait()


def combine_kernel(
    sums, mass, ids, out, load, sums_here, mass_here, ids_scalar, whole, in_sem, out_sem
):
    rows_count = sums.shape[0]
    list_blocks = load.shape[0]
    copies = [
        pltpu.make_async_copy(ids.at[:, 0:1, :], ids_scalar, in_sem.at[0]),
        pltpu.make_async_copy(mass, mass_here, in_sem.at[1]),
    ]
    copies += [
        pltpu.make_async_copy(sums.at[j], sums_here.at[j], in_sem.at[2 + j]) for j in range(rows_count)
    ]
    for copy in copies:
        copy.start()

    def clear(block, carry):
        whole[block] = jnp.zeros(whole.shape[1:], F32)
        return carry

    lax.fori_loop(0, list_blocks, clear, 0)
    for copy in copies:
        copy.wait()
    local = [
        (j, use, lax.rem(ids_scalar[j, 0, USE * j + use], list_blocks))
        for j in range(rows_count)
        for use in range(USE)
    ]

    def one(block, carry):
        total = jnp.zeros((1, CB), F32)
        for j, use, named in local:
            hit = named == block

            @pl.when(hit)
            def _():
                whole[block] += sums_here[j, use * CB : (use + 1) * CB, :].astype(F32)

            total = total + jnp.where(hit, mass_here[j, use : use + 1, :], 0.0)
        load[pl.ds(block, 1), :] = total
        pltpu.make_async_copy(whole.at[block], out.at[block], out_sem.at[block]).start()
        return carry

    lax.fori_loop(0, list_blocks, one, 0)
    for block in range(list_blocks):
        pltpu.make_async_copy(whole.at[block], out.at[block], out_sem.at[block]).wait()


def body(groups, centroids, row_weight, block_ids, block_counts):
    rows_count = lax.axis_size("rows")
    cents_count = lax.axis_size("cents")
    row_blocks = block_ids.shape[0]
    list_blocks = centroids.shape[0] // CB
    list_total = list_blocks * CB * rows_count * cents_count
    distinct = rows_count * USE
    wide = rows_count * distinct
    any_space = pl.BlockSpec(memory_space=pl.ANY)
    vmem = pl.BlockSpec(memory_space=pltpu.VMEM)
    dma = pltpu.SemaphoreType.DMA
    row_total = row_blocks * RB
    sums, mass, all_ids = pl.pallas_call(
        functools.partial(main_kernel, rows_count, cents_count, list_total),
        out_shape=(
            jax.ShapeDtypeStruct((rows_count, USE * CB, D), BF16),
            jax.ShapeDtypeStruct((rows_count, 8, CB), F32),
            jax.ShapeDtypeStruct((rows_count, 8, wide), jnp.int32),
        ),
        in_specs=[any_space, any_space, vmem, vmem, pl.BlockSpec(memory_space=pltpu.SMEM)],
        out_specs=(any_space, vmem, vmem),
        scratch_shapes=[
            pltpu.VMEM((row_total, D), BF16),
            pltpu.VMEM((list_blocks, CB, D), BF16),
            pltpu.VMEM((rows_count, USE * CB, D), BF16),
            pltpu.VMEM((rows_count, USE * CB, D), BF16),
            pltpu.VMEM((row_blocks, rows_count, RB, CB), F32),
            pltpu.VMEM((USE * CB, row_total), BF16),
            pltpu.VMEM((row_total, CB), F32),
            pltpu.VMEM((row_total, CB), F32),
            pltpu.VMEM((8, wide), jnp.int32),
            pltpu.VMEM((distinct, wide), jnp.int32),
            pltpu.VMEM((row_blocks, rows_count, RB), F32),
            pltpu.VMEM((row_blocks, rows_count, CB), F32),
            pltpu.VMEM((distinct, 8, CB), F32),
            pltpu.SMEM((rows_count, 1, wide), jnp.int32),
            pltpu.VMEM((ITERS, distinct + 8, CB), F32),
            pltpu.VMEM((ITERS, rows_count, distinct + 8, CB), F32),
            pltpu.VMEM((distinct, CB), F32),
            pltpu.VMEM((distinct, wide), F32),
            pltpu.VMEM((rows_count, 8, CB), F32),
            pltpu.VMEM((8, CB), F32),
            pltpu.VMEM((cents_count, 8, CB), F32),
            pltpu.VMEM((8, CB), F32),
            dma((3,)),
            dma((rows_count,)), dma((rows_count,)),
            dma((rows_count,)), dma((rows_count,)),
            dma((ITERS, rows_count)), dma((ITERS, rows_count)),
            dma((rows_count,)), dma((rows_count,)),
            dma((rows_count,)), dma((rows_count,)),
            dma((cents_count,)), dma((cents_count,)),
        ],
        compiler_params=pltpu.CompilerParams(
            collective_id=0, has_side_effects=True, vmem_limit_bytes=56 * 2**20
        ),
        cost_estimate=pl.CostEstimate(
            flops=8 * row_total * D * distinct * CB // 2, bytes_accessed=16 * 2**20, transcendentals=0
        ),
        name="assign",
    )(groups, centroids.reshape(list_blocks, CB, D), row_weight.reshape(-1, 128),
      block_ids, block_counts)
    out, load = pl.pallas_call(
        combine_kernel,
        out_shape=(
            jax.ShapeDtypeStruct((list_blocks, CB, D), F32),
            jax.ShapeDtypeStruct((list_blocks, CB), F32),
        ),
        in_specs=[any_space, any_space, any_space],
        out_specs=(any_space, vmem),
        scratch_shapes=[
            pltpu.VMEM((rows_count, USE * CB, D), BF16),
            pltpu.VMEM((rows_count, 8, CB), F32),
            pltpu.SMEM((rows_count, 1, wide), jnp.int32),
            pltpu.VMEM((list_blocks, CB, D), F32),
            dma((2 + rows_count,)),
            dma((list_blocks,)),
        ],
        compiler_params=pltpu.CompilerParams(vmem_limit_bytes=56 * 2**20),
        name="combine",
    )(sums, mass, all_ids)
    return out.reshape(-1, D), load.reshape(-1)


def solution(mesh):
    placed = (
        P(("rows", "cents"), None),
        P(("rows", "cents"), None),
        P(("rows", "cents")),
        P(("rows", "cents"), None),
        P(("rows", "cents")),
    )
    return jax.shard_map(
        body,
        mesh=mesh,
        in_specs=placed,
        out_specs=(P(("rows", "cents"), None), P(("rows", "cents"))),
        check_vma=False,
    )
```

```python
import functools

import jax
import jax.numpy as jnp
from jax import lax
from jax.experimental import pallas as pl
from jax.experimental.pallas import tpu as pltpu
from jax.sharding import PartitionSpec as P

D = 1024
RB = 256
CB = 128
USE = 2
ITERS = 3
BETA = 32.0
EPSILON = 1e-06
PRIOR = 0.25
MESH = pl.DeviceIdType.MESH
F32 = jnp.float32
BF16 = jnp.bfloat16


def normalize(values):
    widened = values.astype(F32)
    factor = lax.rsqrt(jnp.mean(widened * widened, axis=-1, keepdims=True) + EPSILON)
    return (widened * factor).astype(BF16)


def flipped(index, offset):
    result = index
    bit = 1
    while bit <= offset:
        if offset & bit:
            result = result + bit * (1 - 2 * ((index // bit) % 2))
        bit *= 2
    return result


def peer_order(rows_count):
    half = rows_count // 2
    quarter = half // 2
    far = list(range(half + quarter, rows_count)) + list(range(half, half + quarter))
    return far, list(range(half - 1, 0, -1))


def main_kernel(
    rows_count, cents_count, list_total,
    groups, centroids, weights, block_ids, block_counts,
    sums_out, mass_out, ids_out,
    rows, lists, send, lists_in, kernel, left, weight_column, row_scale,
    id_message, id_column, use_table, live_table, column_parts,
    ids_scalar, parts, parts_in, scales, match, mass_send, weight_send, weight_in, total,
    load_sem, ids_send_sem, ids_recv_sem, list_send_sem, list_recv_sem, part_send_sem, part_recv_sem,
    sum_send_sem, sum_recv_sem, mass_send_sem, mass_recv_sem, weight_send_sem, weight_recv_sem,
):
    me = lax.axis_index("rows")
    cent = lax.axis_index("cents")
    distinct = rows_count * USE
    list_blocks = lists.shape[0]
    row_blocks = rows.shape[0] // RB
    far, near = peer_order(rows_count)
    order = far + near
    peers = {j: (flipped(me, j), cent) for j in order}
    cent_peers = {q: (me, (cent + q) % cents_count) for q in range(1, cents_count)}

    load_lists = pltpu.make_async_copy(centroids, lists, load_sem.at[0])
    load_lists.start()
    load_rows = pltpu.make_async_copy(groups, rows, load_sem.at[1])
    load_rows.start()

    barrier = pltpu.get_barrier_semaphore()
    for peer in list(peers.values()) + list(cent_peers.values()):
        pl.semaphore_signal(barrier, inc=1, device_id=peer, device_id_type=MESH)

    ids = block_ids[...]
    slot = lax.broadcasted_iota(jnp.int32, ids.shape, 1)
    block_row = lax.broadcasted_iota(jnp.int32, ids.shape, 0)
    count = jnp.zeros(ids.shape, jnp.int32)
    for block in range(row_blocks):
        count = jnp.where(block_row == block, block_counts[block], count)
    alive = slot < count
    place = lax.broadcasted_iota(jnp.int32, id_message.shape, 1) % distinct
    message = jnp.zeros(id_message.shape, jnp.int32)
    for j in range(rows_count):
        base = (flipped(me, j) * cents_count + cent) * list_blocks
        inside = (ids >= base) & (ids < base + list_blocks)
        named = jnp.max(jnp.where(inside, ids - base, -1), axis=1, keepdims=True)
        live = jnp.max(jnp.where(inside & alive, 1.0, 0.0), axis=1, keepdims=True)
        low = jnp.min(jnp.where(named >= 0, named, list_blocks), axis=0, keepdims=True)
        high = jnp.max(named, axis=0, keepdims=True)
        uses = jnp.broadcast_to((named == high).astype(F32), (row_blocks, RB))
        lives = jnp.broadcast_to(live, (row_blocks, CB))
        for block in range(row_blocks):
            use_table[block, j : j + 1, :] = uses[block : block + 1, :]
            live_table[block, j : j + 1, :] = lives[block : block + 1, :]
        for use, picked in enumerate((low, high)):
            message = jnp.where(place == USE * j + use, base + picked, message)
            row = USE * j + use
            id_column[row : row + 1, :] = jnp.broadcast_to(base + picked, (1, id_column.shape[1]))
    id_message[...] = message

    pl.semaphore_wait(barrier, len(peers) + len(cent_peers))

    def remote(source, target, send_sem, recv_sem, peer):
        copy = pltpu.make_async_remote_copy(
            src_ref=source, dst_ref=target, send_sem=send_sem, recv_sem=recv_sem,
            device_id=peer, device_id_type=MESH,
        )
        copy.start()
        return copy

    id_copies = [
        remote(id_message, ids_out.at[j], ids_send_sem.at[j], ids_recv_sem.at[j], peers[j])
        for j in order
    ]
    ids_out[0] = id_message[...]
    weight_send[...] = jnp.broadcast_to(jnp.sum(weights[...], keepdims=True), weight_send.shape)
    weight_copies = [
        remote(weight_send, weight_in.at[q], weight_send_sem.at[q], weight_recv_sem.at[q], cent_peers[q])
        for q in cent_peers
    ]
    for copy in id_copies:
        copy.wait_recv()
    to_scalar = pltpu.make_async_copy(ids_out.at[:, 0:1, :], ids_scalar, load_sem.at[2])
    to_scalar.start()
    to_scalar.wait()
    load_lists.wait()

    def normalized_list(j, use):
        wanted = lax.rem(ids_scalar[j, 0, USE * j + use], list_blocks)
        return normalize(lists[wanted])

    list_copies = {}

    def start_lists(j):
        list_copies[j] = remote(
            send.at[j], lists_in.at[j], list_send_sem.at[j], list_recv_sem.at[j], peers[j]
        )

    ahead = max(len(far) - 1, 1)
    for j in far[:ahead] + near + far[ahead:]:
        for use in range(USE):
            send[j, use * CB : (use + 1) * CB, :] = normalized_list(j, use)
        if j in near or j in far[:ahead]:
            start_lists(j)
    own_ids = [lax.rem(ids_scalar[0, 0, use], list_blocks) for use in range(USE)]
    for use in range(USE):
        lists_in[0, use * CB : (use + 1) * CB, :] = normalize(lists[own_ids[use]])

    load_rows.wait()

    def normalize_rows(index, carry):
        where = pl.ds(pl.multiple_of(index * CB, CB), CB)
        rows[where, :] = normalize(rows[where, :])
        return carry

    lax.fori_loop(0, row_blocks * RB // CB, normalize_rows, 0)

    for index in range(weights.shape[0]):
        spread = jnp.broadcast_to(weights[index : index + 1, :], (128, 128))
        weight_column[index * 128 : (index + 1) * 128, :] = spread.T

    wide = id_column.shape[1]
    lane = lax.broadcasted_iota(jnp.int32, (1, wide), 1)
    id_row = jnp.zeros((1, wide), jnp.int32)
    for j in range(rows_count):
        id_row = id_row + jnp.where(lane // distinct == j, ids_out[j, 0:1, :], 0)
    same = (id_column[...] == id_row).astype(F32).astype(BF16)
    for term in range(3):
        match[:, term * wide : (term + 1) * wide] = same

    for copy in weight_copies:
        copy.wait_recv()
    group_weight = weight_send[...]
    for q in cent_peers:
        group_weight = group_weight + weight_in[q]
    scales[...] = jnp.ones_like(scales)
    parts[...] = jnp.zeros_like(parts)
    parts[0, distinct : distinct + 8, :] = group_weight

    def scores_of(j):
        def one(block, carry):
            where = pl.ds(pl.multiple_of(block * RB, RB), RB)
            both = lax.dot_general(
                rows[where, :], lists_in[j], (((1,), (1,)), ((), ())), preferred_element_type=F32
            )
            use = use_table[block, j : j + 1, :CB]
            picked = jnp.where(use > 0.5, both[:, CB:], both[:, :CB])
            kernel[block, j] = jnp.exp(picked * (BETA / D)) * live_table[block, j : j + 1, :]
            return carry

        lax.fori_loop(0, row_blocks, one, 0, unroll=2)

    scores_of(0)
    for j in near:
        list_copies[j].wait_recv()
        scores_of(j)
    for index, j in enumerate(far):
        list_copies[j].wait_send()
        if index + ahead < len(far):
            start_lists(far[index + ahead])
        list_copies[j].wait_recv()
        scores_of(j)

    def scale_of(block, j):
        use = use_table[block, j : j + 1, :CB]
        return jnp.where(use > 0.5, scales[USE * j + 1 : USE * j + 2, :], scales[USE * j : USE * j + 1, :])

    def row_step(block):
        total_row = jnp.zeros((RB, CB), F32)
        for j in range(rows_count):
            total_row = total_row + kernel[block, j] * scale_of(block, j)
        where = pl.ds(pl.multiple_of(block * RB, RB), RB)
        return weight_column[where, :] / jnp.sum(total_row, axis=1, keepdims=True)

    part_copies = []
    for step in range(ITERS):
        def column_step(block, carry):
            factor = row_step(block)
            for j in range(rows_count):
                column = jnp.sum((kernel[block, j] * factor).reshape(RB // 8, 8, CB), axis=0)
                use = use_table[block, j : j + 1, :CB]
                column_parts[USE * j] += column * (1.0 - use)
                column_parts[USE * j + 1] += column * use
            return carry

        column_parts[...] = jnp.zeros_like(column_parts)
        lax.fori_loop(0, row_blocks, column_step, 0, unroll=4)
        parts[step, :distinct, :] = jnp.sum(column_parts[...], axis=1)
        copies = [
            remote(
                parts.at[step], parts_in.at[step, j],
                part_send_sem.at[step, j], part_recv_sem.at[step, j], peers[j],
            )
            for j in order
        ]
        parts_in[step, 0] = parts[step]
        for copy in copies:
            copy.wait_recv()
        part_copies += copies
        if step == 0:
            mass = parts_in[0, 0, distinct : distinct + 8, :]
            for j in range(1, rows_count):
                mass = mass + parts_in[0, j, distinct : distinct + 8, :]
            total[...] = mass / list_total
        arrived = parts_in[step, :, :distinct, :].reshape(rows_count * distinct, CB)
        first = arrived.astype(BF16)
        rest = arrived - first.astype(F32)
        second = rest.astype(BF16)
        third = (rest - second.astype(F32)).astype(BF16)
        column_all = jnp.dot(
            match[...], jnp.concatenate([first, second, third], axis=0), preferred_element_type=F32
        )
        target = total[0:1, :]
        scales[...] = target / (column_all + PRIOR * target)

    def last_rows(block, carry):
        where = pl.ds(pl.multiple_of(block * RB, RB), RB)
        row_scale[where, :] = row_step(block)
        return carry

    lax.fori_loop(0, row_blocks, last_rows, 0, unroll=4)

    sum_copies = []
    mass_copies = []
    keep = []
    for j in order + [0]:
        if j in near:
            list_copies[j].wait_send()
        mass_send[j] = jnp.zeros((8, CB), F32)

        def transport_of(block, carry):
            where = pl.ds(pl.multiple_of(block * RB, RB), RB)
            transport = row_scale[where, :] * kernel[block, j] * scale_of(block, j)
            column = jnp.sum(transport, axis=0, keepdims=True)
            use = use_table[block, j : j + 1, :]
            mass_send[j, 0:1, :] += column * (1.0 - use[:, :CB])
            mass_send[j, 1:2, :] += column * use[:, :CB]
            turned = transport.T
            left[:CB, where] = jnp.where(use > 0.5, 0.0, turned).astype(BF16)
            left[CB:, where] = jnp.where(use > 0.5, turned, 0.0).astype(BF16)
            return carry

        lax.fori_loop(0, row_blocks, transport_of, 0, unroll=2)
        mass_send[j] = mass_send[j] / total[...]

        def product(chunk, carry):
            where = pl.ds(pl.multiple_of(chunk * 256, 256), 256)
            send[j, :, where] = jnp.dot(
                left[...], rows[:, where], preferred_element_type=F32
            ).astype(BF16)
            return carry

        lax.fori_loop(0, D // 256, product, 0)
        if j:
            sum_copies.append(
                remote(send.at[j], sums_out.at[j], sum_send_sem.at[j], sum_recv_sem.at[j], peers[j])
            )
            mass_copies.append(
                remote(
                    mass_send.at[j], mass_out.at[j], mass_send_sem.at[j], mass_recv_sem.at[j], peers[j]
                )
            )
        else:
            mass_out[0] = mass_send[0]
            own = pltpu.make_async_copy(send.at[0], sums_out.at[0], load_sem.at[0])
            own.start()
            keep.append(own)

    for copy in id_copies + weight_copies + part_copies:
        copy.wait_send()
    for copy in mass_copies + sum_copies:
        copy.wait()
    for copy in keep:
        copy.wait()


def combine_kernel(
    sums, mass, ids, out, load, sums_here, mass_here, ids_scalar, whole, in_sem, out_sem
):
    rows_count = sums.shape[0]
    list_blocks = load.shape[0]
    copies = [
        pltpu.make_async_copy(ids.at[:, 0:1, :], ids_scalar, in_sem.at[0]),
        pltpu.make_async_copy(mass, mass_here, in_sem.at[1]),
    ]
    copies += [
        pltpu.make_async_copy(sums.at[j], sums_here.at[j], in_sem.at[2 + j]) for j in range(rows_count)
    ]
    for copy in copies:
        copy.start()

    def clear(block, carry):
        whole[block] = jnp.zeros(whole.shape[1:], F32)
        return carry

    lax.fori_loop(0, list_blocks, clear, 0)
    for copy in copies:
        copy.wait()
    local = [
        (j, use, lax.rem(ids_scalar[j, 0, USE * j + use], list_blocks))
        for j in range(rows_count)
        for use in range(USE)
    ]

    def one(block, carry):
        total = jnp.zeros((1, CB), F32)
        for j, use, named in local:
            hit = named == block

            @pl.when(hit)
            def _():
                whole[block] += sums_here[j, use * CB : (use + 1) * CB, :].astype(F32)

            total = total + jnp.where(hit, mass_here[j, use : use + 1, :], 0.0)
        load[pl.ds(block, 1), :] = total
        pltpu.make_async_copy(whole.at[block], out.at[block], out_sem.at[block]).start()
        return carry

    lax.fori_loop(0, list_blocks, one, 0)
    for block in range(list_blocks):
        pltpu.make_async_copy(whole.at[block], out.at[block], out_sem.at[block]).wait()


def body(groups, centroids, row_weight, block_ids, block_counts):
    rows_count = lax.axis_size("rows")
    cents_count = lax.axis_size("cents")
    row_blocks = block_ids.shape[0]
    list_blocks = centroids.shape[0] // CB
    list_total = list_blocks * CB * rows_count * cents_count
    distinct = rows_count * USE
    wide = rows_count * distinct
    any_space = pl.BlockSpec(memory_space=pl.ANY)
    vmem = pl.BlockSpec(memory_space=pltpu.VMEM)
    dma = pltpu.SemaphoreType.DMA
    row_total = row_blocks * RB
    sums, mass, all_ids = pl.pallas_call(
        functools.partial(main_kernel, rows_count, cents_count, list_total),
        out_shape=(
            jax.ShapeDtypeStruct((rows_count, USE * CB, D), BF16),
            jax.ShapeDtypeStruct((rows_count, 8, CB), F32),
            jax.ShapeDtypeStruct((rows_count, 8, wide), jnp.int32),
        ),
        in_specs=[any_space, any_space, vmem, vmem, pl.BlockSpec(memory_space=pltpu.SMEM)],
        out_specs=(any_space, vmem, vmem),
        scratch_shapes=[
            pltpu.VMEM((row_total, D), BF16),
            pltpu.VMEM((list_blocks, CB, D), BF16),
            pltpu.VMEM((rows_count, USE * CB, D), BF16),
            pltpu.VMEM((rows_count, USE * CB, D), BF16),
            pltpu.VMEM((row_blocks, rows_count, RB, CB), F32),
            pltpu.VMEM((USE * CB, row_total), BF16),
            pltpu.VMEM((row_total, CB), F32),
            pltpu.VMEM((row_total, CB), F32),
            pltpu.VMEM((8, wide), jnp.int32),
            pltpu.VMEM((distinct, wide), jnp.int32),
            pltpu.VMEM((row_blocks, rows_count, RB), F32),
            pltpu.VMEM((row_blocks, rows_count, CB), F32),
            pltpu.VMEM((distinct, 8, CB), F32),
            pltpu.SMEM((rows_count, 1, wide), jnp.int32),
            pltpu.VMEM((ITERS, distinct + 8, CB), F32),
            pltpu.VMEM((ITERS, rows_count, distinct + 8, CB), F32),
            pltpu.VMEM((distinct, CB), F32),
            pltpu.VMEM((distinct, 3 * wide), BF16),
            pltpu.VMEM((rows_count, 8, CB), F32),
            pltpu.VMEM((8, CB), F32),
            pltpu.VMEM((cents_count, 8, CB), F32),
            pltpu.VMEM((8, CB), F32),
            dma((3,)),
            dma((rows_count,)), dma((rows_count,)),
            dma((rows_count,)), dma((rows_count,)),
            dma((ITERS, rows_count)), dma((ITERS, rows_count)),
            dma((rows_count,)), dma((rows_count,)),
            dma((rows_count,)), dma((rows_count,)),
            dma((cents_count,)), dma((cents_count,)),
        ],
        compiler_params=pltpu.CompilerParams(
            collective_id=0, has_side_effects=True, vmem_limit_bytes=56 * 2**20
        ),
        cost_estimate=pl.CostEstimate(
            flops=8 * row_total * D * distinct * CB // 2, bytes_accessed=16 * 2**20, transcendentals=0
        ),
        name="assign",
    )(groups, centroids.reshape(list_blocks, CB, D), row_weight.reshape(-1, 128),
      block_ids, block_counts)
    out, load = pl.pallas_call(
        combine_kernel,
        out_shape=(
            jax.ShapeDtypeStruct((list_blocks, CB, D), F32),
            jax.ShapeDtypeStruct((list_blocks, CB), F32),
        ),
        in_specs=[any_space, any_space, any_space],
        out_specs=(any_space, vmem),
        scratch_shapes=[
            pltpu.VMEM((rows_count, USE * CB, D), BF16),
            pltpu.VMEM((rows_count, 8, CB), F32),
            pltpu.SMEM((rows_count, 1, wide), jnp.int32),
            pltpu.VMEM((list_blocks, CB, D), F32),
            dma((2 + rows_count,)),
            dma((list_blocks,)),
        ],
        compiler_params=pltpu.CompilerParams(vmem_limit_bytes=56 * 2**20),
        name="combine",
    )(sums, mass, all_ids)
    return out.reshape(-1, D), load.reshape(-1)


def solution(mesh):
    placed = (
        P(("rows", "cents"), None),
        P(("rows", "cents"), None),
        P(("rows", "cents")),
        P(("rows", "cents"), None),
        P(("rows", "cents")),
    )
    return jax.shard_map(
        body,
        mesh=mesh,
        in_specs=placed,
        out_specs=(P(("rows", "cents"), None), P(("rows", "cents"))),
        check_vma=False,
    )
```

```python
import functools

import jax
import jax.numpy as jnp
from jax import lax
from jax.experimental import pallas as pl
from jax.experimental.pallas import tpu as pltpu
from jax.sharding import PartitionSpec as P

D = 1024
RB = 256
CB = 128
USE = 2
ITERS = 3
BETA = 32.0
EPSILON = 1e-06
PRIOR = 0.25
MESH = pl.DeviceIdType.MESH
F32 = jnp.float32
BF16 = jnp.bfloat16


def normalize(values):
    widened = values.astype(F32)
    factor = lax.rsqrt(jnp.mean(widened * widened, axis=-1, keepdims=True) + EPSILON)
    return (widened * factor).astype(BF16)


def flipped(index, offset):
    result = index
    bit = 1
    while bit <= offset:
        if offset & bit:
            result = result + bit * (1 - 2 * ((index // bit) % 2))
        bit *= 2
    return result


def peer_order(rows_count):
    half = rows_count // 2
    quarter = half // 2
    far = list(range(half + quarter, rows_count)) + list(range(half, half + quarter))
    return far, list(range(half - 1, 0, -1))


def main_kernel(
    rows_count, cents_count, list_total,
    groups, centroids, weights, block_ids, block_counts,
    sums_out, mass_out, ids_out,
    rows, lists, send, lists_in, kernel, left, weight_column, row_scale,
    id_message, id_column, use_table, live_table, column_parts,
    ids_scalar, parts, parts_in, scales, match, mass_send, weight_send, weight_in, total,
    load_sem, ids_send_sem, ids_recv_sem, list_send_sem, list_recv_sem, part_send_sem, part_recv_sem,
    sum_send_sem, sum_recv_sem, mass_send_sem, mass_recv_sem, weight_send_sem, weight_recv_sem,
):
    me = lax.axis_index("rows")
    cent = lax.axis_index("cents")
    distinct = rows_count * USE
    list_blocks = lists.shape[0]
    row_blocks = rows.shape[0] // RB
    far, near = peer_order(rows_count)
    order = far + near
    peers = {j: (flipped(me, j), cent) for j in order}
    cent_peers = {q: (me, (cent + q) % cents_count) for q in range(1, cents_count)}

    load_lists = pltpu.make_async_copy(centroids, lists, load_sem.at[0])
    load_lists.start()
    load_rows = pltpu.make_async_copy(groups, rows, load_sem.at[1])
    load_rows.start()

    barrier = pltpu.get_barrier_semaphore()
    for peer in list(peers.values()) + list(cent_peers.values()):
        pl.semaphore_signal(barrier, inc=1, device_id=peer, device_id_type=MESH)

    ids = block_ids[...]
    slot = lax.broadcasted_iota(jnp.int32, ids.shape, 1)
    block_row = lax.broadcasted_iota(jnp.int32, ids.shape, 0)
    count = jnp.zeros(ids.shape, jnp.int32)
    for block in range(row_blocks):
        count = jnp.where(block_row == block, block_counts[block], count)
    alive = slot < count
    place = lax.broadcasted_iota(jnp.int32, id_message.shape, 1) % distinct
    message = jnp.zeros(id_message.shape, jnp.int32)
    for j in range(rows_count):
        base = (flipped(me, j) * cents_count + cent) * list_blocks
        inside = (ids >= base) & (ids < base + list_blocks)
        named = jnp.max(jnp.where(inside, ids - base, -1), axis=1, keepdims=True)
        live = jnp.max(jnp.where(inside & alive, 1.0, 0.0), axis=1, keepdims=True)
        low = jnp.min(jnp.where(named >= 0, named, list_blocks), axis=0, keepdims=True)
        high = jnp.max(named, axis=0, keepdims=True)
        uses = jnp.broadcast_to((named == high).astype(F32), (row_blocks, RB))
        lives = jnp.broadcast_to(live, (row_blocks, CB))
        for block in range(row_blocks):
            use_table[block, j : j + 1, :] = uses[block : block + 1, :]
            live_table[block, j : j + 1, :] = lives[block : block + 1, :]
        for use, picked in enumerate((low, high)):
            message = jnp.where(place == USE * j + use, base + picked, message)
            row = USE * j + use
            id_column[row : row + 1, :] = jnp.broadcast_to(base + picked, (1, id_column.shape[1]))
    id_message[...] = message

    pl.semaphore_wait(barrier, len(peers) + len(cent_peers))

    def remote(source, target, send_sem, recv_sem, peer):
        copy = pltpu.make_async_remote_copy(
            src_ref=source, dst_ref=target, send_sem=send_sem, recv_sem=recv_sem,
            device_id=peer, device_id_type=MESH,
        )
        copy.start()
        return copy

    id_copies = [
        remote(id_message, ids_out.at[j], ids_send_sem.at[j], ids_recv_sem.at[j], peers[j])
        for j in order
    ]
    ids_out[0] = id_message[...]
    weight_send[...] = jnp.broadcast_to(jnp.sum(weights[...], keepdims=True), weight_send.shape)
    weight_copies = [
        remote(weight_send, weight_in.at[q], weight_send_sem.at[q], weight_recv_sem.at[q], cent_peers[q])
        for q in cent_peers
    ]
    for copy in id_copies:
        copy.wait_recv()
    to_scalar = pltpu.make_async_copy(ids_out.at[:, 0:1, :], ids_scalar, load_sem.at[2])
    to_scalar.start()
    to_scalar.wait()
    load_lists.wait()

    def normalized_list(j, use):
        wanted = lax.rem(ids_scalar[j, 0, USE * j + use], list_blocks)
        return normalize(lists[wanted])

    list_copies = {}

    def start_lists(j):
        list_copies[j] = remote(
            send.at[j], lists_in.at[j], list_send_sem.at[j], list_recv_sem.at[j], peers[j]
        )

    ahead = len(far)
    for j in far[:ahead] + near + far[ahead:]:
        for use in range(USE):
            send[j, use * CB : (use + 1) * CB, :] = normalized_list(j, use)
        if j in near or j in far[:ahead]:
            start_lists(j)
    own_ids = [lax.rem(ids_scalar[0, 0, use], list_blocks) for use in range(USE)]
    for use in range(USE):
        lists_in[0, use * CB : (use + 1) * CB, :] = normalize(lists[own_ids[use]])

    load_rows.wait()

    def normalize_rows(index, carry):
        where = pl.ds(pl.multiple_of(index * CB, CB), CB)
        rows[where, :] = normalize(rows[where, :])
        return carry

    lax.fori_loop(0, row_blocks * RB // CB, normalize_rows, 0)

    for index in range(weights.shape[0]):
        spread = jnp.broadcast_to(weights[index : index + 1, :], (128, 128))
        weight_column[index * 128 : (index + 1) * 128, :] = spread.T

    wide = id_column.shape[1]
    lane = lax.broadcasted_iota(jnp.int32, (1, wide), 1)
    id_row = jnp.zeros((1, wide), jnp.int32)
    for j in range(rows_count):
        id_row = id_row + jnp.where(lane // distinct == j, ids_out[j, 0:1, :], 0)
    same = (id_column[...] == id_row).astype(F32).astype(BF16)
    for term in range(3):
        match[:, term * wide : (term + 1) * wide] = same

    for copy in weight_copies:
        copy.wait_recv()
    group_weight = weight_send[...]
    for q in cent_peers:
        group_weight = group_weight + weight_in[q]
    scales[...] = jnp.ones_like(scales)
    parts[...] = jnp.zeros_like(parts)
    parts[0, distinct : distinct + 8, :] = group_weight

    def scores_of(j):
        def one(block, carry):
            where = pl.ds(pl.multiple_of(block * RB, RB), RB)
            both = lax.dot_general(
                rows[where, :], lists_in[j], (((1,), (1,)), ((), ())), preferred_element_type=F32
            )
            use = use_table[block, j : j + 1, :CB]
            picked = jnp.where(use > 0.5, both[:, CB:], both[:, :CB])
            kernel[block, j] = jnp.exp(picked * (BETA / D)) * live_table[block, j : j + 1, :]
            return carry

        lax.fori_loop(0, row_blocks, one, 0, unroll=2)

    scores_of(0)
    for j in near:
        list_copies[j].wait_recv()
        scores_of(j)
    for index, j in enumerate(far):
        list_copies[j].wait_send()
        if index + ahead < len(far):
            start_lists(far[index + ahead])
        list_copies[j].wait_recv()
        scores_of(j)

    def scale_of(block, j):
        use = use_table[block, j : j + 1, :CB]
        return jnp.where(use > 0.5, scales[USE * j + 1 : USE * j + 2, :], scales[USE * j : USE * j + 1, :])

    def row_step(block):
        total_row = jnp.zeros((RB, CB), F32)
        for j in range(rows_count):
            total_row = total_row + kernel[block, j] * scale_of(block, j)
        where = pl.ds(pl.multiple_of(block * RB, RB), RB)
        return weight_column[where, :] / jnp.sum(total_row, axis=1, keepdims=True)

    part_copies = []
    for step in range(ITERS):
        def column_step(block, carry):
            factor = row_step(block)
            for j in range(rows_count):
                column = jnp.sum((kernel[block, j] * factor).reshape(RB // 8, 8, CB), axis=0)
                use = use_table[block, j : j + 1, :CB]
                column_parts[USE * j] += column * (1.0 - use)
                column_parts[USE * j + 1] += column * use
            return carry

        column_parts[...] = jnp.zeros_like(column_parts)
        lax.fori_loop(0, row_blocks, column_step, 0, unroll=4)
        parts[step, :distinct, :] = jnp.sum(column_parts[...], axis=1)
        copies = [
            remote(
                parts.at[step], parts_in.at[step, j],
                part_send_sem.at[step, j], part_recv_sem.at[step, j], peers[j],
            )
            for j in order
        ]
        parts_in[step, 0] = parts[step]
        for copy in copies:
            copy.wait_recv()
        part_copies += copies
        if step == 0:
            mass = parts_in[0, 0, distinct : distinct + 8, :]
            for j in range(1, rows_count):
                mass = mass + parts_in[0, j, distinct : distinct + 8, :]
            total[...] = mass / list_total
        arrived = parts_in[step, :, :distinct, :].reshape(rows_count * distinct, CB)
        first = arrived.astype(BF16)
        rest = arrived - first.astype(F32)
        second = rest.astype(BF16)
        third = (rest - second.astype(F32)).astype(BF16)
        column_all = jnp.dot(
            match[...], jnp.concatenate([first, second, third], axis=0), preferred_element_type=F32
        )
        target = total[0:1, :]
        scales[...] = target / (column_all + PRIOR * target)

    def last_rows(block, carry):
        where = pl.ds(pl.multiple_of(block * RB, RB), RB)
        row_scale[where, :] = row_step(block)
        return carry

    lax.fori_loop(0, row_blocks, last_rows, 0, unroll=4)

    sum_copies = []
    mass_copies = []
    keep = []
    for j in order + [0]:
        if j in near:
            list_copies[j].wait_send()
        mass_send[j] = jnp.zeros((8, CB), F32)

        def transport_of(block, carry):
            where = pl.ds(pl.multiple_of(block * RB, RB), RB)
            transport = row_scale[where, :] * kernel[block, j] * scale_of(block, j)
            column = jnp.sum(transport, axis=0, keepdims=True)
            use = use_table[block, j : j + 1, :]
            mass_send[j, 0:1, :] += column * (1.0 - use[:, :CB])
            mass_send[j, 1:2, :] += column * use[:, :CB]
            turned = transport.T
            left[:CB, where] = jnp.where(use > 0.5, 0.0, turned).astype(BF16)
            left[CB:, where] = jnp.where(use > 0.5, turned, 0.0).astype(BF16)
            return carry

        lax.fori_loop(0, row_blocks, transport_of, 0, unroll=2)
        mass_send[j] = mass_send[j] / total[...]

        def product(chunk, carry):
            where = pl.ds(pl.multiple_of(chunk * 256, 256), 256)
            send[j, :, where] = jnp.dot(
                left[...], rows[:, where], preferred_element_type=F32
            ).astype(BF16)
            return carry

        lax.fori_loop(0, D // 256, product, 0)
        if j:
            sum_copies.append(
                remote(send.at[j], sums_out.at[j], sum_send_sem.at[j], sum_recv_sem.at[j], peers[j])
            )
            mass_copies.append(
                remote(
                    mass_send.at[j], mass_out.at[j], mass_send_sem.at[j], mass_recv_sem.at[j], peers[j]
                )
            )
        else:
            mass_out[0] = mass_send[0]
            own = pltpu.make_async_copy(send.at[0], sums_out.at[0], load_sem.at[0])
            own.start()
            keep.append(own)

    for copy in id_copies + weight_copies + part_copies:
        copy.wait_send()
    for copy in mass_copies + sum_copies:
        copy.wait()
    for copy in keep:
        copy.wait()


def combine_kernel(
    sums, mass, ids, out, load, sums_here, mass_here, ids_scalar, whole, in_sem, out_sem
):
    rows_count = sums.shape[0]
    list_blocks = load.shape[0]
    copies = [
        pltpu.make_async_copy(ids.at[:, 0:1, :], ids_scalar, in_sem.at[0]),
        pltpu.make_async_copy(mass, mass_here, in_sem.at[1]),
    ]
    copies += [
        pltpu.make_async_copy(sums.at[j], sums_here.at[j], in_sem.at[2 + j]) for j in range(rows_count)
    ]
    for copy in copies:
        copy.start()

    def clear(block, carry):
        whole[block] = jnp.zeros(whole.shape[1:], F32)
        return carry

    lax.fori_loop(0, list_blocks, clear, 0)
    for copy in copies:
        copy.wait()
    local = [
        (j, use, lax.rem(ids_scalar[j, 0, USE * j + use], list_blocks))
        for j in range(rows_count)
        for use in range(USE)
    ]

    def one(block, carry):
        total = jnp.zeros((1, CB), F32)
        for j, use, named in local:
            hit = named == block

            @pl.when(hit)
            def _():
                whole[block] += sums_here[j, use * CB : (use + 1) * CB, :].astype(F32)

            total = total + jnp.where(hit, mass_here[j, use : use + 1, :], 0.0)
        load[pl.ds(block, 1), :] = total
        pltpu.make_async_copy(whole.at[block], out.at[block], out_sem.at[block]).start()
        return carry

    lax.fori_loop(0, list_blocks, one, 0)
    for block in range(list_blocks):
        pltpu.make_async_copy(whole.at[block], out.at[block], out_sem.at[block]).wait()


def body(groups, centroids, row_weight, block_ids, block_counts):
    rows_count = lax.axis_size("rows")
    cents_count = lax.axis_size("cents")
    row_blocks = block_ids.shape[0]
    list_blocks = centroids.shape[0] // CB
    list_total = list_blocks * CB * rows_count * cents_count
    distinct = rows_count * USE
    wide = rows_count * distinct
    any_space = pl.BlockSpec(memory_space=pl.ANY)
    vmem = pl.BlockSpec(memory_space=pltpu.VMEM)
    dma = pltpu.SemaphoreType.DMA
    row_total = row_blocks * RB
    sums, mass, all_ids = pl.pallas_call(
        functools.partial(main_kernel, rows_count, cents_count, list_total),
        out_shape=(
            jax.ShapeDtypeStruct((rows_count, USE * CB, D), BF16),
            jax.ShapeDtypeStruct((rows_count, 8, CB), F32),
            jax.ShapeDtypeStruct((rows_count, 8, wide), jnp.int32),
        ),
        in_specs=[any_space, any_space, vmem, vmem, pl.BlockSpec(memory_space=pltpu.SMEM)],
        out_specs=(any_space, vmem, vmem),
        scratch_shapes=[
            pltpu.VMEM((row_total, D), BF16),
            pltpu.VMEM((list_blocks, CB, D), BF16),
            pltpu.VMEM((rows_count, USE * CB, D), BF16),
            pltpu.VMEM((rows_count, USE * CB, D), BF16),
            pltpu.VMEM((row_blocks, rows_count, RB, CB), F32),
            pltpu.VMEM((USE * CB, row_total), BF16),
            pltpu.VMEM((row_total, CB), F32),
            pltpu.VMEM((row_total, CB), F32),
            pltpu.VMEM((8, wide), jnp.int32),
            pltpu.VMEM((distinct, wide), jnp.int32),
            pltpu.VMEM((row_blocks, rows_count, RB), F32),
            pltpu.VMEM((row_blocks, rows_count, CB), F32),
            pltpu.VMEM((distinct, 8, CB), F32),
            pltpu.SMEM((rows_count, 1, wide), jnp.int32),
            pltpu.VMEM((ITERS, distinct + 8, CB), F32),
            pltpu.VMEM((ITERS, rows_count, distinct + 8, CB), F32),
            pltpu.VMEM((distinct, CB), F32),
            pltpu.VMEM((distinct, 3 * wide), BF16),
            pltpu.VMEM((rows_count, 8, CB), F32),
            pltpu.VMEM((8, CB), F32),
            pltpu.VMEM((cents_count, 8, CB), F32),
            pltpu.VMEM((8, CB), F32),
            dma((3,)),
            dma((rows_count,)), dma((rows_count,)),
            dma((rows_count,)), dma((rows_count,)),
            dma((ITERS, rows_count)), dma((ITERS, rows_count)),
            dma((rows_count,)), dma((rows_count,)),
            dma((rows_count,)), dma((rows_count,)),
            dma((cents_count,)), dma((cents_count,)),
        ],
        compiler_params=pltpu.CompilerParams(
            collective_id=0, has_side_effects=True, vmem_limit_bytes=56 * 2**20
        ),
        cost_estimate=pl.CostEstimate(
            flops=8 * row_total * D * distinct * CB // 2, bytes_accessed=16 * 2**20, transcendentals=0
        ),
        name="assign",
    )(groups, centroids.reshape(list_blocks, CB, D), row_weight.reshape(-1, 128),
      block_ids, block_counts)
    out, load = pl.pallas_call(
        combine_kernel,
        out_shape=(
            jax.ShapeDtypeStruct((list_blocks, CB, D), F32),
            jax.ShapeDtypeStruct((list_blocks, CB), F32),
        ),
        in_specs=[any_space, any_space, any_space],
        out_specs=(any_space, vmem),
        scratch_shapes=[
            pltpu.VMEM((rows_count, USE * CB, D), BF16),
            pltpu.VMEM((rows_count, 8, CB), F32),
            pltpu.SMEM((rows_count, 1, wide), jnp.int32),
            pltpu.VMEM((list_blocks, CB, D), F32),
            dma((2 + rows_count,)),
            dma((list_blocks,)),
        ],
        compiler_params=pltpu.CompilerParams(vmem_limit_bytes=56 * 2**20),
        name="combine",
    )(sums, mass, all_ids)
    return out.reshape(-1, D), load.reshape(-1)


def solution(mesh):
    placed = (
        P(("rows", "cents"), None),
        P(("rows", "cents"), None),
        P(("rows", "cents")),
        P(("rows", "cents"), None),
        P(("rows", "cents")),
    )
    return jax.shard_map(
        body,
        mesh=mesh,
        in_specs=placed,
        out_specs=(P(("rows", "cents"), None), P(("rows", "cents"))),
        check_vma=False,
    )
```
